32 devices in a mesh: dp: 16 (over z, y, x), tensor: 2 (over core).
Axes of the slice: x: 2, y: 2, z: 4, core: 2. Of those that a mesh axis runs over, the one named last changes fastest.
Arguments:
- tokens: bfloat16 [32768, 768], P(('dp', 'tensor')), may hold values from -6 to 6
- out_cot: bfloat16 [32768, 768], P(('dp', 'tensor')), may hold values from -6 to 6
- norm_gain: bfloat16 [2, 768], replicated, may hold values from 0.5 to 1.5
- norm_bias: bfloat16 [2, 768], replicated, may hold values from -1.25 to 1.25
- qkv_weight: bfloat16 [3, 768, 768], P(None, None, 'tensor'), may hold values from -0.21875 to 0.21875
- qkv_bias: bfloat16 [3, 768], P(None, 'tensor'), may hold values from -1.25 to 1.25
- out_weight: bfloat16 [768, 768], P('tensor'), may hold values from -1.75 to 1.75
- out_bias: bfloat16 [2, 768], replicated, may hold values from -1.25 to 1.25
- up_weight: bfloat16 [768, 3072], P(None, 'tensor'), may hold values from -0.21875 to 0.21875
- up_bias: bfloat16 [3072], P('tensor'), may hold values from -1.25 to 1.25
- down_weight: bfloat16 [3072, 768], P('tensor'), may hold values from -0.109375 to 0.109375
- seq_lengths: int32 [64], replicated, may hold values from 1 to 1024, as said below
- seq_owner: int32 [64], replicated, may hold values from 0 to 15, as said below
Outputs:
- mixed: bfloat16 [32768, 768], P(('dp', 'tensor'))
- tokens_grad: bfloat16 [32768, 768], P(('dp', 'tensor'))
- norm_gain_grad: float32 [2, 768], replicated
- norm_bias_grad: float32 [2, 768], replicated
- qkv_weight_grad: float32 [3, 768, 768], P(None, None, 'tensor')
- qkv_bias_grad: float32 [3, 768], P(None, 'tensor')
- out_weight_grad: float32 [768, 768], P('tensor')
- out_bias_grad: float32 [2, 768], replicated
- up_weight_grad: float32 [768, 3072], P(None, 'tensor')
- up_bias_grad: float32 [3072], P('tensor')
- down_weight_grad: float32 [3072, 768], P('tensor')
The draws below stay inside these ranges and needn't reach their ends.
Inputs may be any that keep to these rules, and one draw needn't show every extreme that they name: `seq_lengths`: each entry is the length of one sequence; at least one equals 1024. `seq_owner`: each data index holds exactly 4 sequences, laid out in list order from its slot 0; their lengths sum to at most 2048, exactly 2048 on at least one index; on every index the first sequence ends before slot 1024 and the second reaches past it.
All inputs are finite; a program needn't handle non-finite values.
Results may differ from the reference program's by a relative error of at most 0.01.
Values may be sent and summed in bfloat16 or wider, within the bound.
A program may use at most 256 MiB of HBM per device.

```python
import math
import jax
import jax.numpy as jnp
from jax import lax

D = 768
H = 12
HD = 64
ROT = 16
FF = 3072
MAXLEN = 1024
SEQ_DEV = 4
SLOTS = 2048
NSEQ = 64
TOKENS = 32768
N_DP = 16


def plan(key):
    count = NSEQ // SEQ_DEV
    keys = jax.random.split(key, 6)
    first = jax.random.randint(keys[0], (count,), MAXLEN // 4, 7 * MAXLEN // 8 + 1)
    second = jax.random.randint(keys[1], (count,), MAXLEN + 1 - first, MAXLEN + 1)
    fullest = jax.random.randint(keys[2], (), 0, count)
    chosen = jnp.arange(count) == fullest
    second = jnp.where(chosen, MAXLEN, second)
    remain = 2 * MAXLEN - first - second
    third = jax.random.randint(keys[3], (count,), 1, remain)
    fourth = jax.random.randint(keys[4], (count,), 1, remain - third + 1)
    fourth = jnp.where(chosen, remain - third, fourth)
    table = jnp.stack([first, second, third, fourth], 1)
    owner = jax.random.permutation(keys[5], jnp.repeat(jnp.arange(count), 4))
    order = jnp.arange(count * 4)
    earlier = (owner[:, None] == owner[None, :]) & (order[None, :] < order[:, None])
    rank = jnp.sum(earlier.astype(jnp.int32), 1)
    lengths = table[owner, rank]
    return (lengths.astype(jnp.int32), owner.astype(jnp.int32))


def draw_seq_lengths(key, part):
    lengths, owner = plan(key)
    return lengths


def draw_seq_owner(key, part):
    lengths, owner = plan(key)
    return owner


def level_of(own_key, shape, cuts, least, top_value):
    loudness = 1.0
    for dim, parts in cuts:
        heights = jax.random.uniform(jax.random.fold_in(jax.random.fold_in(own_key, 6), dim), (parts,), jnp.float32, least / len(cuts), top_value / len(cuts))
        loudness = loudness * jnp.repeat(jnp.exp(heights), shape[dim] // parts).reshape((-1,) + (1,) * (len(shape) - 1 - dim))
    return loudness


def noise(stream_key, shape, width, bound, pieces=(), kind=jnp.bfloat16):
    level = level_of(stream_key, shape, pieces, -0.22, 0.18) if pieces else 1.0
    entries = jax.random.normal(stream_key, shape, jnp.float32) * width * level
    return jnp.minimum(jnp.maximum(entries, -bound), bound).astype(kind)


def setup_inputs(seed: int = 0) -> dict:
    key_list = jax.random.split(jax.random.key(seed), 14)
    tokens = noise(key_list[0], (TOKENS, D), 1.0, 6.0, ((0, 32),))
    out_cot = noise(key_list[1], (TOKENS, D), 1.0, 6.0, ((0, 32),))
    norm_gain = jnp.clip(1.0 + 0.1 * jax.random.normal(key_list[2], (2, D), jnp.float32), 0.5, 1.5).astype(jnp.bfloat16)
    norm_bias = noise(key_list[3], (2, D), 0.2, 1.25)
    qkv_weight = noise(key_list[4], (3, D, D), D ** -0.5, 0.21875, ((2, 2),))
    qkv_bias = noise(key_list[5], (3, D), 0.2, 1.25, ((1, 2),))
    out_weight = noise(key_list[6], (D, D), (max(D // 64, 1)) ** -0.5, 1.75, ((0, 2),))
    out_bias = noise(key_list[7], (2, D), 0.2, 1.25)
    up_weight = noise(key_list[8], (D, FF), D ** -0.5, 0.21875, ((1, 2),))
    up_bias = noise(key_list[9], (FF,), 0.2, 1.25, ((0, 2),))
    down_weight = noise(key_list[10], (FF, D), FF ** -0.5, 0.109375, ((0, 2),))
    seq_lengths = draw_seq_lengths(jax.random.fold_in(key_list[13], 71), 0)
    seq_owner = draw_seq_owner(jax.random.fold_in(key_list[13], 71), 0)
    return {"tokens": tokens, "out_cot": out_cot, "norm_gain": norm_gain, "norm_bias": norm_bias, "qkv_weight": qkv_weight, "qkv_bias": qkv_bias, "out_weight": out_weight, "out_bias": out_bias, "up_weight": up_weight, "up_bias": up_bias, "down_weight": down_weight, "seq_lengths": seq_lengths, "seq_owner": seq_owner}


@jax.custom_vjp
def low(v):
    return lax.optimization_barrier(v.astype(jnp.bfloat16)).astype(jnp.float32)

@jax.custom_vjp
def low_back(v):
    return v

def low_keep(v):
    return (low(v), None)

def low_pass(kept, grad):
    return (grad,)

def back_keep(v):
    return (v, None)

def back_low(kept, grad):
    return (low(grad),)
low.defvjp(low_keep, low_pass)
low_back.defvjp(back_keep, back_low)

def normalize(values, gain, shift):
    center = values - lax.optimization_barrier(jnp.mean(values, -1, keepdims=True))
    spread = lax.optimization_barrier(jnp.mean(center * center, -1, keepdims=True))
    return center * lax.rsqrt(spread + 1e-05) * gain + shift

def layout(lengths, owners, index, slot_count):
    mine = owners == index
    sizes = jnp.where(mine, lengths, 0).astype(jnp.int32)
    starts = jnp.cumsum(sizes).astype(jnp.int32) - sizes
    rows = jnp.arange(slot_count, dtype=jnp.int32)
    covers = mine[None, :] & (starts[None, :] <= rows[:, None])
    counter = lax.optimization_barrier(jnp.sum(covers.astype(jnp.int32), 1))
    begins = lax.optimization_barrier(jnp.max(jnp.where(covers, starts[None, :], 0), 1))
    filled = rows < jnp.sum(sizes)
    segment = jnp.where(filled, counter, lengths.shape[0] + 1 + rows)
    places = jnp.where(filled, rows - begins, 0)
    return (segment.astype(jnp.int32), places.astype(jnp.int32), filled)

def rotary(values, places):
    half = ROT // 2
    freq = 10000.0 ** (-jnp.arange(half, dtype=jnp.float32) * 2.0 / ROT)
    angles = places.astype(jnp.float32)[:, None] * freq[None, :]
    angles = jnp.concatenate([angles, angles], 1)
    cosine = jnp.cos(angles)[:, None, :]
    sine = jnp.sin(angles)[:, None, :]
    turned = values[..., :ROT]
    swapped = jnp.concatenate([-turned[..., half:], turned[..., :half]], -1)
    return jnp.concatenate([turned * cosine + swapped * sine, values[..., ROT:]], -1)

def attend(query, keyset, values, segment):
    block_rows = min(512, MAXLEN)
    window = MAXLEN + block_rows
    scale = 1.0 / math.sqrt(HD)
    front = jnp.zeros((MAXLEN,) + keyset.shape[1:], jnp.float32)
    key_pad = jnp.concatenate([front, keyset], 0)
    value_pad = jnp.concatenate([front, values], 0)
    segment_pad = jnp.concatenate([jnp.full((MAXLEN,), -1, jnp.int32), segment], 0)

    def one_block(offset):
        rows_q = lax.dynamic_slice_in_dim(query, offset, block_rows, 0)
        rows_k = lax.dynamic_slice_in_dim(key_pad, offset, window, 0)
        rows_v = lax.dynamic_slice_in_dim(value_pad, offset, window, 0)
        seg_q = lax.dynamic_slice_in_dim(segment, offset, block_rows, 0)
        seg_k = lax.dynamic_slice_in_dim(segment_pad, offset, window, 0)
        allowed = (seg_q[:, None] == seg_k[None, :]) & (jnp.arange(window)[None, :] - MAXLEN <= jnp.arange(block_rows)[:, None])
        scores = jnp.einsum('qhd,khd->hqk', rows_q, rows_k, precision=lax.Precision.HIGHEST) * scale
        scores = low_back(jnp.where(allowed[None], scores, -1e+30))
        weights = low(jax.nn.softmax(scores, axis=-1))
        return jnp.einsum('hqk,khd->qhd', weights, rows_v, precision=lax.Precision.HIGHEST)
    offsets = jnp.arange(0, query.shape[0], block_rows, dtype=jnp.int32)
    outputs = lax.map(jax.checkpoint(one_block), offsets)
    return outputs.reshape(query.shape)

def forward(x, weights, segment, places):
    norm_gain, norm_bias, qkv_weight, qkv_bias, out_weight, out_bias, up_weight, up_bias, down_weight = weights
    count = x.shape[0]
    first = low(normalize(x, norm_gain[0], norm_bias[0]))
    second = low(normalize(x, norm_gain[1], norm_bias[1]))
    mixed_qkv = low_back(jnp.einsum('sd,cde->cse', first, qkv_weight, precision=lax.Precision.HIGHEST) + qkv_bias[:, None, :])
    split = mixed_qkv.reshape(3, count, H, HD)
    query = low(rotary(split[0], places))
    keyset = low(rotary(split[1], places))
    values = low(split[2])
    attended = low(low_back(attend(query, keyset, values, segment).reshape(count, D)))
    branch = jnp.dot(attended, out_weight, precision=lax.Precision.HIGHEST)
    hidden = low_back(jnp.dot(second, up_weight, precision=lax.Precision.HIGHEST) + up_bias)
    active = low(jax.nn.gelu(hidden, approximate=False))
    branch = branch + jnp.dot(active, down_weight, precision=lax.Precision.HIGHEST)
    return x + branch + out_bias[0] + out_bias[1]

def reference(tokens, out_cot, norm_gain, norm_bias, qkv_weight, qkv_bias, out_weight, out_bias, up_weight, up_bias, down_weight, seq_lengths, seq_owner):
    params = tuple((item.astype(jnp.float32) for item in (norm_gain, norm_bias, qkv_weight, qkv_bias, out_weight, out_bias, up_weight, up_bias, down_weight)))

    def group(carry, index):
        offset = index * SLOTS
        x = lax.dynamic_slice_in_dim(tokens, offset, SLOTS, 0).astype(jnp.float32)
        cot = lax.dynamic_slice_in_dim(out_cot, offset, SLOTS, 0).astype(jnp.float32)
        segment, places, filled = layout(seq_lengths, seq_owner, index, SLOTS)

        def run(x_in, *weights):
            return forward(x_in, weights, segment, places)
        result, pull = jax.vjp(run, x, *params)
        grads = pull(cot * filled[:, None].astype(jnp.float32))
        carry = tuple((total + part for total, part in zip(carry, grads[1:])))
        return (carry, (result.astype(jnp.bfloat16), grads[0].astype(jnp.bfloat16)))
    start_sums = tuple((jnp.zeros_like(item) for item in params))
    sums, (mixed, back) = lax.scan(group, start_sums, jnp.arange(N_DP, dtype=jnp.int32))
    return (mixed.reshape(-1, D), back.reshape(-1, D), sums[0], sums[1], sums[2], sums[3], sums[4], sums[5], sums[6], sums[7], sums[8])
```

```python
import functools
import math

import jax
import jax.numpy as jnp
from jax import lax
from jax.experimental import pallas as pl
from jax.experimental.pallas import tpu as pltpu
from jax.sharding import PartitionSpec as P

HD = 64
ROT = 16
MAXLEN = 1024
BLOCK = 256
PAIR = 2 * HD
ROWS = 512
F32 = jnp.float32
BF16 = jnp.bfloat16


def standard(values):
    center = values - jnp.mean(values, -1, keepdims=True)
    spread = jnp.mean(center * center, -1, keepdims=True)
    inverse = lax.rsqrt(spread + 1e-05)
    return (center * inverse, inverse)


def layout(lengths, owners, index, slot_count):
    mine = owners == index
    sizes = jnp.where(mine, lengths, 0)
    starts = jnp.cumsum(sizes) - sizes
    rows = jnp.arange(slot_count, dtype=jnp.int32)
    covers = mine[None, :] & (starts[None, :] <= rows[:, None])
    begins = jnp.max(jnp.where(covers, starts[None, :], 0), 1)
    filled = rows < jnp.sum(sizes)
    return (jnp.where(filled, begins, rows), filled)


def rotary_tables(places):
    half = ROT // 2
    freq = 10000.0 ** (-jnp.arange(half, dtype=F32) * 2.0 / ROT)
    angles = places.astype(F32)[:, None] * freq[None, :]
    angles = jnp.concatenate([angles, angles], 1)
    rest = jnp.zeros((places.shape[0], HD - ROT), F32)
    cosine = jnp.concatenate([jnp.cos(angles), rest + 1.0], 1)
    sine = jnp.concatenate([jnp.sin(angles), rest], 1)
    return jnp.concatenate([cosine] * 2, 1), jnp.concatenate([sine] * 2, 1)


def dot(a, b, dims):
    return lax.dot_general(a, b, (dims, ((), ())), preferred_element_type=F32)


NN = ((1,), (0,))
NT = ((1,), (1,))
TN = ((0,), (0,))


def attention_kernel(
    low_ref, a_ref, back_ref, start_ref, cos_ref, sin_ref,
    o_ref, da_ref,
    q_s, k_s, v_s, dk_s, dv_s, s_s, dp_s, q2_s, do2_s, top_s, sum_s, mix_s, o2_s, dq2_s,
):
    slots = q_s.shape[0]
    blocks = slots // BLOCK
    lane = lax.broadcasted_iota(jnp.int32, (BLOCK, PAIR), 1)
    within = lane % HD

    def turn(w):
        up = pltpu.roll(w, PAIR - ROT // 2, 1)
        down = pltpu.roll(w, ROT // 2, 1)
        return jnp.where(within < ROT // 2, -up, down)

    def prepare(b, carry):
        rows = pl.ds(pl.multiple_of(b * BLOCK, BLOCK), BLOCK)
        cosine = cos_ref[rows, :]
        sine = sin_ref[rows, :]
        q = a_ref[0, rows, :]
        k = a_ref[1, rows, :]
        q = (q * cosine + turn(q) * sine).astype(BF16)
        q_s[rows, :] = (q.astype(F32) * (1.0 / math.sqrt(HD))).astype(BF16)
        k_s[rows, :] = (k * cosine + turn(k) * sine).astype(BF16)
        v_s[rows, :] = a_ref[2, rows, :].astype(BF16)
        dk_s[rows, :] = jnp.zeros((BLOCK, PAIR), F32)
        dv_s[rows, :] = jnp.zeros((BLOCK, PAIR), F32)
        return carry

    lax.fori_loop(0, blocks, prepare, 0)

    def query_block(i, carry):
        rows = pl.ds(pl.multiple_of(i * BLOCK, BLOCK), BLOCK)
        low = low_ref[i]
        none = jnp.zeros((BLOCK, PAIR), BF16)
        q = q_s[rows, :]
        back = back_ref[rows, :]
        q2_s[:BLOCK, :] = jnp.where(lane < HD, q, none)
        q2_s[BLOCK:, :] = jnp.where(lane < HD, none, q)
        do2_s[:BLOCK, :] = jnp.where(lane < HD, back, none)
        do2_s[BLOCK:, :] = jnp.where(lane < HD, none, back)
        start = start_ref[rows, :]
        start2 = jnp.concatenate([start, start], 0)
        row = lax.broadcasted_iota(jnp.int32, (BLOCK, 1), 0) + i * BLOCK
        row2 = jnp.concatenate([row, row], 0)
        top_s[...] = jnp.full(top_s.shape, -1e30, F32)
        sum_s[...] = jnp.zeros(sum_s.shape, F32)
        mix_s[...] = jnp.zeros(mix_s.shape, F32)
        o2_s[...] = jnp.zeros(o2_s.shape, F32)
        dq2_s[...] = jnp.zeros(dq2_s.shape, F32)
        column = lax.broadcasted_iota(jnp.int32, (2 * BLOCK, BLOCK), 1)

        def score(j, c):
            keys = pl.ds(pl.multiple_of(j * BLOCK, BLOCK), BLOCK)
            s = dot(q2_s[...], k_s[keys, :], NT)
            place = column + j * BLOCK
            s = jnp.where((place >= start2) & (place <= row2), s, -1e30)
            s_s[j - low] = s
            dp_s[j - low] = dot(do2_s[...], v_s[keys, :], NT)
            top_s[...] = jnp.maximum(top_s[...], jnp.maximum(s[:, :128], s[:, 128:]))
            return c

        lax.fori_loop(low, i + 1, score, 0)
        top = jnp.max(top_s[...], -1, keepdims=True)

        def expand(j, c):
            p = jnp.exp(s_s[j - low] - top)
            s_s[j - low] = p
            m = p * dp_s[j - low]
            sum_s[...] += p[:, :128] + p[:, 128:]
            mix_s[...] += m[:, :128] + m[:, 128:]
            return c

        lax.fori_loop(low, i + 1, expand, 0)
        total = jnp.sum(sum_s[...], -1, keepdims=True)
        inverse = 1.0 / total
        inner = jnp.sum(mix_s[...], -1, keepdims=True) * inverse

        def apply(j, c):
            keys = pl.ds(pl.multiple_of(j * BLOCK, BLOCK), BLOCK)
            p = s_s[j - low] * inverse
            ds = (p * (dp_s[j - low] - inner)).astype(BF16)
            p = p.astype(BF16)
            o2_s[...] += dot(p, v_s[keys, :], NN)
            dq2_s[...] += dot(ds, k_s[keys, :], NN)
            dk_s[keys, :] += dot(ds, q2_s[...], TN)
            dv_s[keys, :] += dot(p, do2_s[...], TN)
            return c

        lax.fori_loop(low, i + 1, apply, 0)
        o_ref[rows, :] = jnp.where(lane < HD, o2_s[:BLOCK, :], o2_s[BLOCK:, :]).astype(BF16)
        dq = jnp.where(lane < HD, dq2_s[:BLOCK, :], dq2_s[BLOCK:, :]) * (1.0 / math.sqrt(HD))
        da_ref[0, rows, :] = (dq * cos_ref[rows, :] - turn(dq) * sin_ref[rows, :]).astype(BF16)
        return carry

    lax.fori_loop(0, blocks, query_block, 0)

    def finish(b, carry):
        rows = pl.ds(pl.multiple_of(b * BLOCK, BLOCK), BLOCK)
        dk = dk_s[rows, :]
        da_ref[1, rows, :] = (dk * cos_ref[rows, :] - turn(dk) * sin_ref[rows, :]).astype(BF16)
        da_ref[2, rows, :] = dv_s[rows, :].astype(BF16)
        return carry

    lax.fori_loop(0, blocks, finish, 0)


def attention(low, projected, back, start, cosine, sine):
    _, slots, width = projected.shape
    pairs = width // PAIR
    span = MAXLEN // BLOCK + 1
    return pl.pallas_call(
        attention_kernel,
        grid_spec=pltpu.PrefetchScalarGridSpec(
            num_scalar_prefetch=1,
            grid=(pairs,),
            in_specs=[
                pl.BlockSpec((3, slots, PAIR), lambda g, low: (0, 0, g)),
                pl.BlockSpec((slots, PAIR), lambda g, low: (0, g)),
                pl.BlockSpec((slots, 1), lambda g, low: (0, 0)),
                pl.BlockSpec((slots, PAIR), lambda g, low: (0, 0)),
                pl.BlockSpec((slots, PAIR), lambda g, low: (0, 0)),
            ],
            out_specs=[
                pl.BlockSpec((slots, PAIR), lambda g, low: (0, g)),
                pl.BlockSpec((3, slots, PAIR), lambda g, low: (0, 0, g)),
            ],
            scratch_shapes=[
                pltpu.VMEM((slots, PAIR), BF16),
                pltpu.VMEM((slots, PAIR), BF16),
                pltpu.VMEM((slots, PAIR), BF16),
                pltpu.VMEM((slots, PAIR), F32),
                pltpu.VMEM((slots, PAIR), F32),
                pltpu.VMEM((span, 2 * BLOCK, BLOCK), F32),
                pltpu.VMEM((span, 2 * BLOCK, BLOCK), F32),
                pltpu.VMEM((2 * BLOCK, PAIR), BF16),
                pltpu.VMEM((2 * BLOCK, PAIR), BF16),
                pltpu.VMEM((2 * BLOCK, PAIR), F32),
                pltpu.VMEM((2 * BLOCK, PAIR), F32),
                pltpu.VMEM((2 * BLOCK, PAIR), F32),
                pltpu.VMEM((2 * BLOCK, PAIR), F32),
                pltpu.VMEM((2 * BLOCK, PAIR), F32),
            ],
        ),
        out_shape=[
            jax.ShapeDtypeStruct((slots, width), BF16),
            jax.ShapeDtypeStruct((3, slots, width), BF16),
        ],
        compiler_params=pltpu.CompilerParams(vmem_limit_bytes=52 * 2**20),
        cost_estimate=pl.CostEstimate(
            flops=24 * slots * MAXLEN * width, bytes_accessed=24 * slots * width,
            transcendentals=slots * MAXLEN * width // HD,
        ),
        name="attention",
    )(low, projected, back, start, cosine, sine)


def feed_kernel(h_ref, dy_ref, up_ref, bias_ref, down_ref,
                part_ref, dh_ref, dup_ref, dbias_ref, ddown_ref, up_s, down_s, part_s, dh_s):
    slots = h_ref.shape[0]
    step = pl.program_id(0)
    last = pl.num_programs(0) - 1
    up_s[...] = jnp.zeros(up_s.shape, F32)
    down_s[...] = jnp.zeros(down_s.shape, F32)
    dbias_ref[...] = jnp.zeros(dbias_ref.shape, F32)

    @pl.when(step == 0)
    def _():
        part_s[...] = jnp.zeros(part_s.shape, F32)
        dh_s[...] = jnp.zeros(dh_s.shape, F32)

    def body(b, carry):
        rows = pl.ds(pl.multiple_of(b * ROWS, ROWS), ROWS)
        h = h_ref[rows, :]
        dy = dy_ref[rows, :]
        u = dot(h, up_ref[...], NN) + bias_ref[...].astype(F32)
        dg = dot(dy, down_ref[...], NT)
        phi = 0.5 * (1.0 + lax.erf(u * math.sqrt(0.5)))
        g = (u * phi).astype(BF16)
        slope = phi + u * (jnp.exp(-0.5 * (u * u)) * (1.0 / math.sqrt(2.0 * math.pi)))
        du = (slope * dg).astype(BF16)
        part_s[rows, :] += dot(g, down_ref[...], NN)
        down_s[...] += dot(g, dy, TN)
        dh_s[rows, :] += dot(du, up_ref[...], NT)
        up_s[...] += dot(h, du, TN)
        dbias_ref[...] += jnp.sum(du.astype(F32), 0, keepdims=True)
        return carry

    lax.fori_loop(0, slots // ROWS, body, 0)
    dup_ref[...] = up_s[...].astype(dup_ref.dtype)
    ddown_ref[...] = down_s[...].astype(ddown_ref.dtype)

    @pl.when(step == last)
    def _():
        part_ref[...] = part_s[...].astype(part_ref.dtype)
        dh_ref[...] = dh_s[...].astype(dh_ref.dtype)


def feed(h, dy, up, bias, down):
    slots, width = h.shape
    hidden = up.shape[1]
    tile = 256
    whole = lambda t: (0, 0)
    return pl.pallas_call(
        feed_kernel,
        grid=(hidden // tile,),
        in_specs=[
            pl.BlockSpec((slots, width), whole, pipeline_mode=pl.Buffered(1)),
            pl.BlockSpec((slots, width), whole, pipeline_mode=pl.Buffered(1)),
            pl.BlockSpec((width, tile), lambda t: (0, t)),
            pl.BlockSpec((1, tile), lambda t: (0, t)),
            pl.BlockSpec((tile, width), lambda t: (t, 0)),
        ],
        out_specs=[
            pl.BlockSpec((slots, width), whole, pipeline_mode=pl.Buffered(1)),
            pl.BlockSpec((slots, width), whole, pipeline_mode=pl.Buffered(1)),
            pl.BlockSpec((width, tile), lambda t: (0, t)),
            pl.BlockSpec((1, tile), lambda t: (0, t)),
            pl.BlockSpec((tile, width), lambda t: (t, 0)),
        ],
        scratch_shapes=[
            pltpu.VMEM((width, tile), F32),
            pltpu.VMEM((tile, width), F32),
            pltpu.VMEM((slots, width), F32),
            pltpu.VMEM((slots, width), F32),
        ],
        out_shape=[
            jax.ShapeDtypeStruct((slots, width), F32),
            jax.ShapeDtypeStruct((slots, width), F32),
            jax.ShapeDtypeStruct((width, hidden), BF16),
            jax.ShapeDtypeStruct((1, hidden), F32),
            jax.ShapeDtypeStruct((hidden, width), BF16),
        ],
        compiler_params=pltpu.CompilerParams(vmem_limit_bytes=56 * 2**20),
        cost_estimate=pl.CostEstimate(
            flops=12 * slots * width * hidden, bytes_accessed=22 * 2**20,
            transcendentals=2 * slots * hidden,
        ),
        name="feed",
    )(h, dy, up, bias, down)


def shards(
    tokens,
    out_cot,
    norm_gain,
    norm_bias,
    qkv_weight,
    qkv_bias,
    out_weight,
    out_bias,
    up_weight,
    up_bias,
    down_weight,
    seq_lengths,
    seq_owner,
):
    rows_local = tokens.shape[0]
    slots = rows_local * lax.axis_size("tensor")
    half_index = lax.axis_index("tensor")
    start, filled = layout(seq_lengths, seq_owner, lax.axis_index("dp"), slots)
    places = jnp.arange(slots, dtype=jnp.int32) - start
    valid_local = lax.dynamic_slice_in_dim(filled, half_index * rows_local, rows_local, 0)
    gains = norm_gain.astype(F32)
    shifts = norm_bias.astype(F32)
    x = tokens.astype(F32)
    whole_rows = lax.all_gather(tokens, "tensor", axis=0, tiled=True)
    cot_local = out_cot * valid_local[:, None].astype(BF16)
    cot = lax.all_gather(cot_local, "tensor", axis=0, tiled=True)
    unit_rows, inverse_rows = standard(whole_rows.astype(F32))
    first = (unit_rows * gains[0] + shifts[0]).astype(BF16)
    second = (unit_rows * gains[1] + shifts[1]).astype(BF16)

    feed_part, second_back, up_grad, up_bias_grad, down_grad = feed(
        second, cot, up_weight, up_bias[None, :], down_weight
    )
    up_sum, down_sum = lax.psum((up_grad, down_grad), "dp")

    projected = (
        jnp.einsum("sd,cde->cse", first, qkv_weight, preferred_element_type=F32)
        + qkv_bias.astype(F32)[:, None, :]
    )
    attended_back = dot(cot, out_weight, NT).astype(BF16)
    cosine, sine = rotary_tables(places)
    attended, qkv_delta = attention(
        start[::BLOCK] // BLOCK, projected, attended_back, start[:, None], cosine, sine
    )

    partial_value = feed_part + dot(attended, out_weight, NN)
    summed = lax.psum_scatter(
        partial_value.astype(BF16), "tensor", scatter_dimension=0, tiled=True
    ).astype(F32)
    biases = out_bias.astype(F32)
    mixed = (x + summed + biases[0] + biases[1]).astype(BF16)
    out_w_grad = dot(attended, cot, TN)
    qkv_grad = jnp.einsum("sd,cse->cde", first, qkv_delta, preferred_element_type=F32)
    qkv_bias_grad = jnp.sum(qkv_delta.astype(F32), 1)
    first_back = jnp.einsum("cse,cde->sd", qkv_delta, qkv_weight, preferred_element_type=F32)
    combined = gains[0] * first_back + gains[1] * second_back
    combined_sum = lax.psum_scatter(
        combined.astype(BF16), "tensor", scatter_dimension=0, tiled=True
    ).astype(F32)

    gain_grad = jnp.stack(
        [jnp.sum(first_back * unit_rows, 0), jnp.sum(second_back * unit_rows, 0)], 0
    )
    shift_grad = jnp.stack([jnp.sum(first_back, 0), jnp.sum(second_back, 0)], 0)
    bias_grad = jnp.sum(cot_local.astype(F32), 0)

    qkv_grad16, out_grad16, up_sum, down_sum = lax.optimization_barrier(
        (qkv_grad.astype(BF16), out_w_grad.astype(BF16), up_sum, down_sum)
    )
    width = tokens.shape[1]
    shared = jnp.concatenate([gain_grad, shift_grad, bias_grad[None]], 0).reshape(-1)
    shared = lax.psum(shared, "tensor")
    vectors = jnp.concatenate([shared, qkv_bias_grad.reshape(-1), up_bias_grad.reshape(-1)])
    qkv_sum, out_sum, vector_sum = lax.psum((qkv_grad16, out_grad16, vectors), "dp")
    shared_sum = vector_sum[: 5 * width].reshape(5, width)
    qkv_bias_sum = vector_sum[5 * width : 5 * width + qkv_bias.size].reshape(qkv_bias.shape)
    up_bias_sum = vector_sum[5 * width + qkv_bias.size :]

    unit_local = lax.dynamic_slice_in_dim(unit_rows, half_index * rows_local, rows_local, 0)
    inverse_local = lax.dynamic_slice_in_dim(inverse_rows, half_index * rows_local, rows_local, 0)
    average = jnp.mean(combined_sum, -1, keepdims=True)
    along = jnp.mean(combined_sum * unit_local, -1, keepdims=True)
    x_back = inverse_local * (combined_sum - average - unit_local * along)
    tokens_grad = (cot_local.astype(F32) + x_back).astype(BF16)
    return (
        mixed,
        tokens_grad,
        shared_sum[:2],
        shared_sum[2:4],
        qkv_sum.astype(F32),
        qkv_bias_sum,
        out_sum.astype(F32),
        jnp.stack([shared_sum[4], shared_sum[4]], 0),
        up_sum.astype(F32),
        up_bias_sum,
        down_sum.astype(F32),
    )

def solution(mesh):
    return jax.shard_map(
        shards,
        mesh=mesh,
        in_specs=(
            P(("dp", "tensor"), None),
            P(("dp", "tensor"), None),
            P(),
            P(),
            P(None, None, "tensor"),
            P(None, "tensor"),
            P("tensor", None),
            P(),
            P(None, "tensor"),
            P("tensor"),
            P("tensor", None),
            P(),
            P(),
        ),
        out_specs=(
            P(("dp", "tensor"), None),
            P(("dp", "tensor"), None),
            P(),
            P(),
            P(None, None, "tensor"),
            P(None, "tensor"),
            P("tensor", None),
            P(),
            P(None, "tensor"),
            P("tensor"),
            P("tensor", None),
        ),
        check_vma=False,
    )
```

```python
import functools
import math

import jax
import jax.numpy as jnp
from jax import lax
from jax.experimental import pallas as pl
from jax.experimental.pallas import tpu as pltpu
from jax.sharding import PartitionSpec as P

HD = 64
ROT = 16
MAXLEN = 1024
BLOCK = 256
PAIR = 2 * HD
ROWS = 512
F32 = jnp.float32
BF16 = jnp.bfloat16


def standard(values):
    center = values - jnp.mean(values, -1, keepdims=True)
    spread = jnp.mean(center * center, -1, keepdims=True)
    inverse = lax.rsqrt(spread + 1e-05)
    return (center * inverse, inverse)


def layout(lengths, owners, index, slot_count):
    mine = owners == index
    sizes = jnp.where(mine, lengths, 0)
    starts = jnp.cumsum(sizes) - sizes
    rows = jnp.arange(slot_count, dtype=jnp.int32)
    covers = mine[None, :] & (starts[None, :] <= rows[:, None])
    begins = jnp.max(jnp.where(covers, starts[None, :], 0), 1)
    filled = rows < jnp.sum(sizes)
    return (jnp.where(filled, begins, rows), filled)


def rotary_tables(places):
    half = ROT // 2
    freq = 10000.0 ** (-jnp.arange(half, dtype=F32) * 2.0 / ROT)
    angles = places.astype(F32)[:, None] * freq[None, :]
    angles = jnp.concatenate([angles, angles], 1)
    rest = jnp.zeros((places.shape[0], HD - ROT), F32)
    cosine = jnp.concatenate([jnp.cos(angles), rest + 1.0], 1)
    sine = jnp.concatenate([jnp.sin(angles), rest], 1)
    return jnp.concatenate([cosine] * 2, 1), jnp.concatenate([sine] * 2, 1)


def dot(a, b, dims):
    return lax.dot_general(a, b, (dims, ((), ())), preferred_element_type=F32)


NN = ((1,), (0,))
NT = ((1,), (1,))
TN = ((0,), (0,))


def attention_kernel(
    low_ref, a_ref, back_ref, start_ref, cos_ref, sin_ref,
    o_ref, da_ref,
    q_s, k_s, v_s, dk_s, dv_s, s_s, dp_s, q2_s, do2_s, top_s, sum_s, mix_s, o2_s, dq2_s,
):
    slots = q_s.shape[0]
    blocks = slots // BLOCK
    lane = lax.broadcasted_iota(jnp.int32, (BLOCK, PAIR), 1)
    within = lane % HD

    def turn(w):
        up = pltpu.roll(w, PAIR - ROT // 2, 1)
        down = pltpu.roll(w, ROT // 2, 1)
        return jnp.where(within < ROT // 2, -up, down)

    def prepare(b, carry):
        rows = pl.ds(pl.multiple_of(b * BLOCK, BLOCK), BLOCK)
        cosine = cos_ref[rows, :]
        sine = sin_ref[rows, :]
        q = a_ref[0, rows, :]
        k = a_ref[1, rows, :]
        q = (q * cosine + turn(q) * sine).astype(BF16)
        q_s[rows, :] = (q.astype(F32) * (1.0 / math.sqrt(HD))).astype(BF16)
        k_s[rows, :] = (k * cosine + turn(k) * sine).astype(BF16)
        v_s[rows, :] = a_ref[2, rows, :].astype(BF16)
        dk_s[rows, :] = jnp.zeros((BLOCK, PAIR), F32)
        dv_s[rows, :] = jnp.zeros((BLOCK, PAIR), F32)
        return carry

    lax.fori_loop(0, blocks, prepare, 0)

    def query_block(i, carry):
        rows = pl.ds(pl.multiple_of(i * BLOCK, BLOCK), BLOCK)
        low = low_ref[i]
        none = jnp.zeros((BLOCK, PAIR), BF16)
        q = q_s[rows, :]
        back = back_ref[rows, :]
        q2_s[:BLOCK, :] = jnp.where(lane < HD, q, none)
        q2_s[BLOCK:, :] = jnp.where(lane < HD, none, q)
        do2_s[:BLOCK, :] = jnp.where(lane < HD, back, none)
        do2_s[BLOCK:, :] = jnp.where(lane < HD, none, back)
        start = start_ref[rows, :]
        start2 = jnp.concatenate([start, start], 0)
        row = lax.broadcasted_iota(jnp.int32, (BLOCK, 1), 0) + i * BLOCK
        row2 = jnp.concatenate([row, row], 0)
        top_s[...] = jnp.full(top_s.shape, -1e30, F32)
        sum_s[...] = jnp.zeros(sum_s.shape, F32)
        mix_s[...] = jnp.zeros(mix_s.shape, F32)
        o2_s[...] = jnp.zeros(o2_s.shape, F32)
        dq2_s[...] = jnp.zeros(dq2_s.shape, F32)
        column = lax.broadcasted_iota(jnp.int32, (2 * BLOCK, BLOCK), 1)

        def score(j, c):
            keys = pl.ds(pl.multiple_of(j * BLOCK, BLOCK), BLOCK)
            s = dot(q2_s[...], k_s[keys, :], NT)
            place = column + j * BLOCK
            s = jnp.where((place >= start2) & (place <= row2), s, -1e30)
            s_s[j - low] = s
            dp_s[j - low] = dot(do2_s[...], v_s[keys, :], NT)
            top_s[...] = jnp.maximum(top_s[...], jnp.maximum(s[:, :128], s[:, 128:]))
            return c

        lax.fori_loop(low, i + 1, score, 0)
        top = jnp.max(top_s[...], -1, keepdims=True)

        def expand(j, c):
            p = jnp.exp(s_s[j - low] - top)
            s_s[j - low] = p
            m = p * dp_s[j - low]
            sum_s[...] += p[:, :128] + p[:, 128:]
            mix_s[...] += m[:, :128] + m[:, 128:]
            return c

        lax.fori_loop(low, i + 1, expand, 0)
        total = jnp.sum(sum_s[...], -1, keepdims=True)
        inverse = 1.0 / total
        inner = jnp.sum(mix_s[...], -1, keepdims=True) * inverse

        def apply(j, c):
            keys = pl.ds(pl.multiple_of(j * BLOCK, BLOCK), BLOCK)
            p = s_s[j - low] * inverse
            ds = (p * (dp_s[j - low] - inner)).astype(BF16)
            p = p.astype(BF16)
            o2_s[...] += dot(p, v_s[keys, :], NN)
            dq2_s[...] += dot(ds, k_s[keys, :], NN)
            dk_s[keys, :] += dot(ds, q2_s[...], TN)
            dv_s[keys, :] += dot(p, do2_s[...], TN)
            return c

        lax.fori_loop(low, i + 1, apply, 0)
        o_ref[rows, :] = jnp.where(lane < HD, o2_s[:BLOCK, :], o2_s[BLOCK:, :]).astype(BF16)
        dq = jnp.where(lane < HD, dq2_s[:BLOCK, :], dq2_s[BLOCK:, :]) * (1.0 / math.sqrt(HD))
        da_ref[0, rows, :] = (dq * cos_ref[rows, :] - turn(dq) * sin_ref[rows, :]).astype(BF16)
        return carry

    lax.fori_loop(0, blocks, query_block, 0)

    def finish(b, carry):
        rows = pl.ds(pl.multiple_of(b * BLOCK, BLOCK), BLOCK)
        dk = dk_s[rows, :]
        da_ref[1, rows, :] = (dk * cos_ref[rows, :] - turn(dk) * sin_ref[rows, :]).astype(BF16)
        da_ref[2, rows, :] = dv_s[rows, :].astype(BF16)
        return carry

    lax.fori_loop(0, blocks, finish, 0)


def attention(low, projected, back, start, cosine, sine):
    _, slots, width = projected.shape
    pairs = width // PAIR
    span = MAXLEN // BLOCK + 1
    return pl.pallas_call(
        attention_kernel,
        grid_spec=pltpu.PrefetchScalarGridSpec(
            num_scalar_prefetch=1,
            grid=(pairs,),
            in_specs=[
                pl.BlockSpec((3, slots, PAIR), lambda g, low: (0, 0, g)),
                pl.BlockSpec((slots, PAIR), lambda g, low: (0, g)),
                pl.BlockSpec((slots, 1), lambda g, low: (0, 0)),
                pl.BlockSpec((slots, PAIR), lambda g, low: (0, 0)),
                pl.BlockSpec((slots, PAIR), lambda g, low: (0, 0)),
            ],
            out_specs=[
                pl.BlockSpec((slots, PAIR), lambda g, low: (0, g)),
                pl.BlockSpec((3, slots, PAIR), lambda g, low: (0, 0, g)),
            ],
            scratch_shapes=[
                pltpu.VMEM((slots, PAIR), BF16),
                pltpu.VMEM((slots, PAIR), BF16),
                pltpu.VMEM((slots, PAIR), BF16),
                pltpu.VMEM((slots, PAIR), F32),
                pltpu.VMEM((slots, PAIR), F32),
                pltpu.VMEM((span, 2 * BLOCK, BLOCK), F32),
                pltpu.VMEM((span, 2 * BLOCK, BLOCK), F32),
                pltpu.VMEM((2 * BLOCK, PAIR), BF16),
                pltpu.VMEM((2 * BLOCK, PAIR), BF16),
                pltpu.VMEM((2 * BLOCK, PAIR), F32),
                pltpu.VMEM((2 * BLOCK, PAIR), F32),
                pltpu.VMEM((2 * BLOCK, PAIR), F32),
                pltpu.VMEM((2 * BLOCK, PAIR), F32),
                pltpu.VMEM((2 * BLOCK, PAIR), F32),
            ],
        ),
        out_shape=[
            jax.ShapeDtypeStruct((slots, width), BF16),
            jax.ShapeDtypeStruct((3, slots, width), BF16),
        ],
        compiler_params=pltpu.CompilerParams(vmem_limit_bytes=52 * 2**20),
        cost_estimate=pl.CostEstimate(
            flops=24 * slots * MAXLEN * width, bytes_accessed=24 * slots * width,
            transcendentals=slots * MAXLEN * width // HD,
        ),
        name="attention",
    )(low, projected, back, start, cosine, sine)


def feed_kernel(h_ref, dy_ref, up_ref, bias_ref, down_ref,
                part_ref, dh_ref, dup_ref, dbias_ref, ddown_ref, up_s, down_s, part_s, dh_s):
    slots = h_ref.shape[0]
    step = pl.program_id(0)
    last = pl.num_programs(0) - 1
    up_s[...] = jnp.zeros(up_s.shape, F32)
    down_s[...] = jnp.zeros(down_s.shape, F32)
    dbias_ref[...] = jnp.zeros(dbias_ref.shape, F32)

    @pl.when(step == 0)
    def _():
        part_s[...] = jnp.zeros(part_s.shape, F32)
        dh_s[...] = jnp.zeros(dh_s.shape, F32)

    def body(b, carry):
        rows = pl.ds(pl.multiple_of(b * ROWS, ROWS), ROWS)
        h = h_ref[rows, :]
        dy = dy_ref[rows, :]
        u = dot(h, up_ref[...], NN) + bias_ref[...].astype(F32)
        dg = dot(dy, down_ref[...], NT)
        phi = 0.5 * (1.0 + lax.erf(u * math.sqrt(0.5)))
        g = (u * phi).astype(BF16)
        slope = phi + u * (jnp.exp(-0.5 * (u * u)) * (1.0 / math.sqrt(2.0 * math.pi)))
        du = (slope * dg).astype(BF16)
        part_s[rows, :] += dot(g, down_ref[...], NN)
        down_s[...] += dot(g, dy, TN)
        dh_s[rows, :] += dot(du, up_ref[...], NT)
        up_s[...] += dot(h, du, TN)
        dbias_ref[...] += jnp.sum(du.astype(F32), 0, keepdims=True)
        return carry

    lax.fori_loop(0, slots // ROWS, body, 0)
    dup_ref[...] = up_s[...].astype(dup_ref.dtype)
    ddown_ref[...] = down_s[...].astype(ddown_ref.dtype)

    @pl.when(step == last)
    def _():
        part_ref[...] = part_s[...].astype(part_ref.dtype)
        dh_ref[...] = dh_s[...].astype(dh_ref.dtype)


def feed(h, dy, up, bias, down):
    slots, width = h.shape
    hidden = up.shape[1]
    tile = 256
    whole = lambda t: (0, 0)
    return pl.pallas_call(
        feed_kernel,
        grid=(hidden // tile,),
        in_specs=[
            pl.BlockSpec((slots, width), whole, pipeline_mode=pl.Buffered(1)),
            pl.BlockSpec((slots, width), whole, pipeline_mode=pl.Buffered(1)),
            pl.BlockSpec((width, tile), lambda t: (0, t)),
            pl.BlockSpec((1, tile), lambda t: (0, t)),
            pl.BlockSpec((tile, width), lambda t: (t, 0)),
        ],
        out_specs=[
            pl.BlockSpec((slots, width), whole, pipeline_mode=pl.Buffered(1)),
            pl.BlockSpec((slots, width), whole, pipeline_mode=pl.Buffered(1)),
            pl.BlockSpec((width, tile), lambda t: (0, t)),
            pl.BlockSpec((1, tile), lambda t: (0, t)),
            pl.BlockSpec((tile, width), lambda t: (t, 0)),
        ],
        scratch_shapes=[
            pltpu.VMEM((width, tile), F32),
            pltpu.VMEM((tile, width), F32),
            pltpu.VMEM((slots, width), F32),
            pltpu.VMEM((slots, width), F32),
        ],
        out_shape=[
            jax.ShapeDtypeStruct((slots, width), F32),
            jax.ShapeDtypeStruct((slots, width), F32),
            jax.ShapeDtypeStruct((width, hidden), BF16),
            jax.ShapeDtypeStruct((1, hidden), F32),
            jax.ShapeDtypeStruct((hidden, width), BF16),
        ],
        compiler_params=pltpu.CompilerParams(vmem_limit_bytes=56 * 2**20),
        cost_estimate=pl.CostEstimate(
            flops=12 * slots * width * hidden, bytes_accessed=22 * 2**20,
            transcendentals=2 * slots * hidden,
        ),
        name="feed",
    )(h, dy, up, bias, down)


def exchange_kernel(count, x_ref, out_ref, held, total, send_one, recv_one, send_two, recv_two):
    me = lax.axis_index("dp")

    def peer(d):
        return lax.rem(me + d, count)

    barrier = pltpu.get_barrier_semaphore()

    def greet(d, c):
        pl.semaphore_signal(
            barrier, inc=1, device_id={"dp": peer(d)}, device_id_type=pl.DeviceIdType.MESH
        )
        return c

    lax.fori_loop(1, count, greet, 0)
    pl.semaphore_wait(barrier, count - 1)

    def scatter(d):
        return pltpu.make_async_remote_copy(
            src_ref=x_ref.at[peer(d)],
            dst_ref=held.at[d],
            send_sem=send_one.at[d],
            recv_sem=recv_one.at[d],
            device_id={"dp": peer(d)},
            device_id_type=pl.DeviceIdType.MESH,
        )

    def gather(d):
        return pltpu.make_async_remote_copy(
            src_ref=out_ref.at[me],
            dst_ref=out_ref.at[me],
            send_sem=send_two.at[d],
            recv_sem=recv_two.at[d],
            device_id={"dp": peer(d)},
            device_id_type=pl.DeviceIdType.MESH,
        )

    def start_scatter(d, c):
        scatter(d).start()
        return c

    def take(d, c):
        scatter(d).wait_recv()
        total[...] += held[d].astype(F32)
        return c

    def start_gather(d, c):
        gather(d).start()
        return c

    def end(d, c):
        scatter(d).wait_send()
        gather(d).wait_send()
        gather(d).wait_recv()
        return c

    lax.fori_loop(1, count, start_scatter, 0)
    total[...] = x_ref[me].astype(F32)
    lax.fori_loop(1, count, take, 0)
    out_ref[me] = total[...].astype(BF16)
    lax.fori_loop(1, count, start_gather, 0)
    lax.fori_loop(1, count, end, 0)


def exchange(parts):
    count, chunk, cols = parts.shape
    return pl.pallas_call(
        functools.partial(exchange_kernel, count),
        out_shape=jax.ShapeDtypeStruct(parts.shape, BF16),
        in_specs=[pl.BlockSpec(memory_space=pltpu.VMEM)],
        out_specs=pl.BlockSpec(memory_space=pltpu.VMEM),
        scratch_shapes=[
            pltpu.VMEM(parts.shape, BF16),
            pltpu.VMEM((chunk, cols), F32),
            pltpu.SemaphoreType.DMA((count,)),
            pltpu.SemaphoreType.DMA((count,)),
            pltpu.SemaphoreType.DMA((count,)),
            pltpu.SemaphoreType.DMA((count,)),
        ],
        compiler_params=pltpu.CompilerParams(
            collective_id=0, has_side_effects=True, vmem_limit_bytes=32 * 2**20
        ),
        name="exchange",
    )(parts)


def shards(
    tokens,
    out_cot,
    norm_gain,
    norm_bias,
    qkv_weight,
    qkv_bias,
    out_weight,
    out_bias,
    up_weight,
    up_bias,
    down_weight,
    seq_lengths,
    seq_owner,
):
    rows_local = tokens.shape[0]
    slots = rows_local * lax.axis_size("tensor")
    half_index = lax.axis_index("tensor")
    start, filled = layout(seq_lengths, seq_owner, lax.axis_index("dp"), slots)
    places = jnp.arange(slots, dtype=jnp.int32) - start
    valid_local = lax.dynamic_slice_in_dim(filled, half_index * rows_local, rows_local, 0)
    gains = norm_gain.astype(F32)
    shifts = norm_bias.astype(F32)
    x = tokens.astype(F32)
    whole_rows = lax.all_gather(tokens, "tensor", axis=0, tiled=True)
    cot_local = out_cot * valid_local[:, None].astype(BF16)
    cot = lax.all_gather(cot_local, "tensor", axis=0, tiled=True)
    unit_rows, inverse_rows = standard(whole_rows.astype(F32))
    first = (unit_rows * gains[0] + shifts[0]).astype(BF16)
    second = (unit_rows * gains[1] + shifts[1]).astype(BF16)

    feed_part, second_back, up_grad, up_bias_grad, down_grad = feed(
        second, cot, up_weight, up_bias[None, :], down_weight
    )
    up_sum, down_sum = lax.psum((up_grad, down_grad), "dp")

    projected = (
        jnp.einsum("sd,cde->cse", first, qkv_weight, preferred_element_type=F32)
        + qkv_bias.astype(F32)[:, None, :]
    )
    attended_back = dot(cot, out_weight, NT).astype(BF16)
    cosine, sine = rotary_tables(places)
    attended, qkv_delta = attention(
        start[::BLOCK] // BLOCK, projected, attended_back, start[:, None], cosine, sine
    )

    partial_value = feed_part + dot(attended, out_weight, NN)
    summed = lax.psum_scatter(
        partial_value.astype(BF16), "tensor", scatter_dimension=0, tiled=True
    ).astype(F32)
    biases = out_bias.astype(F32)
    mixed = (x + summed + biases[0] + biases[1]).astype(BF16)
    out_w_grad = dot(attended, cot, TN)
    qkv_grad = jnp.einsum("sd,cse->cde", first, qkv_delta, preferred_element_type=F32)
    qkv_bias_grad = jnp.sum(qkv_delta.astype(F32), 1)
    first_back = jnp.einsum("cse,cde->sd", qkv_delta, qkv_weight, preferred_element_type=F32)
    combined = gains[0] * first_back + gains[1] * second_back
    combined_sum = lax.psum_scatter(
        combined.astype(BF16), "tensor", scatter_dimension=0, tiled=True
    ).astype(F32)

    gain_grad = jnp.stack(
        [jnp.sum(first_back * unit_rows, 0), jnp.sum(second_back * unit_rows, 0)], 0
    )
    shift_grad = jnp.stack([jnp.sum(first_back, 0), jnp.sum(second_back, 0)], 0)
    bias_grad = jnp.sum(cot_local.astype(F32), 0)

    width = tokens.shape[1]
    shared = jnp.concatenate([gain_grad, shift_grad, bias_grad[None]], 0).reshape(-1)
    shared = lax.psum(shared, "tensor")
    vectors = jnp.concatenate([shared, qkv_bias_grad.reshape(-1), up_bias_grad.reshape(-1)])
    cols = qkv_grad.shape[2]
    extra = -(-vectors.size // cols)
    vectors = jnp.pad(vectors, (0, extra * cols - vectors.size)).reshape(extra, cols)
    qkv_rows = qkv_grad.shape[0] * qkv_grad.shape[1]
    out_rows = out_w_grad.shape[0]
    pieces = [qkv_grad.reshape(qkv_rows, cols)]
    pieces += [out_w_grad[:, c : c + cols] for c in range(0, width, cols)]
    pieces += [vectors]
    count = lax.axis_size("dp")
    used = sum(piece.shape[0] for piece in pieces)
    chunk = -(-used // (16 * count)) * 16
    pieces += [jnp.zeros((chunk * count - used, cols), F32)]
    joined = jnp.concatenate([piece.astype(BF16) for piece in pieces], 0)
    total = exchange(joined.reshape(count, chunk, cols)).reshape(chunk * count, cols)
    qkv_sum = total[:qkv_rows].reshape(qkv_grad.shape)
    out_sum = jnp.concatenate(
        [
            total[qkv_rows + n * out_rows : qkv_rows + (n + 1) * out_rows]
            for n in range(width // cols)
        ],
        1,
    )
    vector_sum = total[used - extra : used].astype(F32).reshape(-1)
    shared_sum = vector_sum[: 5 * width].reshape(5, width)
    qkv_bias_sum = vector_sum[5 * width : 5 * width + qkv_bias.size].reshape(qkv_bias.shape)
    up_bias_sum = vector_sum[5 * width + qkv_bias.size :][: up_bias.size]

    unit_local = lax.dynamic_slice_in_dim(unit_rows, half_index * rows_local, rows_local, 0)
    inverse_local = lax.dynamic_slice_in_dim(inverse_rows, half_index * rows_local, rows_local, 0)
    average = jnp.mean(combined_sum, -1, keepdims=True)
    along = jnp.mean(combined_sum * unit_local, -1, keepdims=True)
    x_back = inverse_local * (combined_sum - average - unit_local * along)
    tokens_grad = (cot_local.astype(F32) + x_back).astype(BF16)
    return (
        mixed,
        tokens_grad,
        shared_sum[:2],
        shared_sum[2:4],
        qkv_sum.astype(F32),
        qkv_bias_sum,
        out_sum.astype(F32),
        jnp.stack([shared_sum[4], shared_sum[4]], 0),
        up_sum.astype(F32),
        up_bias_sum,
        down_sum.astype(F32),
    )

def solution(mesh):
    return jax.shard_map(
        shards,
        mesh=mesh,
        in_specs=(
            P(("dp", "tensor"), None),
            P(("dp", "tensor"), None),
            P(),
            P(),
            P(None, None, "tensor"),
            P(None, "tensor"),
            P("tensor", None),
            P(),
            P(None, "tensor"),
            P("tensor"),
            P("tensor", None),
            P(),
            P(),
        ),
        out_specs=(
            P(("dp", "tensor"), None),
            P(("dp", "tensor"), None),
            P(),
            P(),
            P(None, None, "tensor"),
            P(None, "tensor"),
            P("tensor", None),
            P(),
            P(None, "tensor"),
            P("tensor"),
            P("tensor", None),
        ),
        check_vma=False,
    )
```

```python
import functools
import math

import jax
import jax.numpy as jnp
from jax import lax
from jax.experimental import pallas as pl
from jax.experimental.pallas import tpu as pltpu
from jax.sharding import PartitionSpec as P

HD = 64
ROT = 16
MAXLEN = 1024
BLOCK = 256
PAIR = 2 * HD
ROWS = 512
F32 = jnp.float32
BF16 = jnp.bfloat16


def standard(values):
    center = values - jnp.mean(values, -1, keepdims=True)
    spread = jnp.mean(center * center, -1, keepdims=True)
    inverse = lax.rsqrt(spread + 1e-05)
    return (center * inverse, inverse)


def layout(lengths, owners, index, slot_count):
    mine = owners == index
    sizes = jnp.where(mine, lengths, 0)
    starts = jnp.cumsum(sizes) - sizes
    rows = jnp.arange(slot_count, dtype=jnp.int32)
    covers = mine[None, :] & (starts[None, :] <= rows[:, None])
    begins = jnp.max(jnp.where(covers, starts[None, :], 0), 1)
    filled = rows < jnp.sum(sizes)
    return (jnp.where(filled, begins, rows), filled)


def rotary_tables(places):
    half = ROT // 2
    freq = 10000.0 ** (-jnp.arange(half, dtype=F32) * 2.0 / ROT)
    angles = places.astype(F32)[:, None] * freq[None, :]
    angles = jnp.concatenate([angles, angles], 1)
    rest = jnp.zeros((places.shape[0], HD - ROT), F32)
    cosine = jnp.concatenate([jnp.cos(angles), rest + 1.0], 1)
    sine = jnp.concatenate([jnp.sin(angles), rest], 1)
    return jnp.concatenate([cosine] * 2, 1), jnp.concatenate([sine] * 2, 1)


def dot(a, b, dims):
    return lax.dot_general(a, b, (dims, ((), ())), preferred_element_type=F32)


NN = ((1,), (0,))
NT = ((1,), (1,))
TN = ((0,), (0,))


def attention_kernel(
    low_ref, a_ref, back_ref, start_ref, cos_ref, sin_ref,
    o_ref, da_ref,
    q_s, k_s, v_s, dk_s, dv_s, s_s, dp_s, q2_s, do2_s, top_s, sum_s, mix_s, o2_s, dq2_s,
):
    slots = q_s.shape[0]
    blocks = slots // BLOCK
    lane = lax.broadcasted_iota(jnp.int32, (BLOCK, PAIR), 1)
    within = lane % HD

    def turn(w):
        up = pltpu.roll(w, PAIR - ROT // 2, 1)
        down = pltpu.roll(w, ROT // 2, 1)
        return jnp.where(within < ROT // 2, -up, down)

    def prepare(b, carry):
        rows = pl.ds(pl.multiple_of(b * BLOCK, BLOCK), BLOCK)
        cosine = cos_ref[rows, :]
        sine = sin_ref[rows, :]
        q = a_ref[0, rows, :]
        k = a_ref[1, rows, :]
        q = (q * cosine + turn(q) * sine).astype(BF16)
        q_s[rows, :] = (q.astype(F32) * (1.0 / math.sqrt(HD))).astype(BF16)
        k_s[rows, :] = (k * cosine + turn(k) * sine).astype(BF16)
        v_s[rows, :] = a_ref[2, rows, :].astype(BF16)
        dk_s[rows, :] = jnp.zeros((BLOCK, PAIR), F32)
        dv_s[rows, :] = jnp.zeros((BLOCK, PAIR), F32)
        return carry

    lax.fori_loop(0, blocks, prepare, 0)

    def query_block(i, carry):
        rows = pl.ds(pl.multiple_of(i * BLOCK, BLOCK), BLOCK)
        low = low_ref[i]
        none = jnp.zeros((BLOCK, PAIR), BF16)
        q = q_s[rows, :]
        back = back_ref[rows, :]
        q2_s[:BLOCK, :] = jnp.where(lane < HD, q, none)
        q2_s[BLOCK:, :] = jnp.where(lane < HD, none, q)
        do2_s[:BLOCK, :] = jnp.where(lane < HD, back, none)
        do2_s[BLOCK:, :] = jnp.where(lane < HD, none, back)
        start = start_ref[rows, :]
        start2 = jnp.concatenate([start, start], 0)
        row = lax.broadcasted_iota(jnp.int32, (BLOCK, 1), 0) + i * BLOCK
        row2 = jnp.concatenate([row, row], 0)
        top_s[...] = jnp.full(top_s.shape, -1e30, F32)
        sum_s[...] = jnp.zeros(sum_s.shape, F32)
        mix_s[...] = jnp.zeros(mix_s.shape, F32)
        o2_s[...] = jnp.zeros(o2_s.shape, F32)
        dq2_s[...] = jnp.zeros(dq2_s.shape, F32)
        column = lax.broadcasted_iota(jnp.int32, (2 * BLOCK, BLOCK), 1)

        def score(j, c):
            keys = pl.ds(pl.multiple_of(j * BLOCK, BLOCK), BLOCK)
            s = dot(q2_s[...], k_s[keys, :], NT)
            place = column + j * BLOCK
            s = jnp.where((place >= start2) & (place <= row2), s, -1e30)
            s_s[j - low] = s
            dp_s[j - low] = dot(do2_s[...], v_s[keys, :], NT)
            top_s[...] = jnp.maximum(top_s[...], jnp.maximum(s[:, :128], s[:, 128:]))
            return c

        lax.fori_loop(low, i + 1, score, 0)
        top = jnp.max(top_s[...], -1, keepdims=True)

        def expand(j, c):
            p = jnp.exp(s_s[j - low] - top)
            s_s[j - low] = p
            m = p * dp_s[j - low]
            sum_s[...] += p[:, :128] + p[:, 128:]
            mix_s[...] += m[:, :128] + m[:, 128:]
            return c

        lax.fori_loop(low, i + 1, expand, 0)
        total = jnp.sum(sum_s[...], -1, keepdims=True)
        inverse = 1.0 / total
        inner = jnp.sum(mix_s[...], -1, keepdims=True) * inverse

        def apply(j, c):
            keys = pl.ds(pl.multiple_of(j * BLOCK, BLOCK), BLOCK)
            p = s_s[j - low] * inverse
            ds = (p * (dp_s[j - low] - inner)).astype(BF16)
            p = p.astype(BF16)
            o2_s[...] += dot(p, v_s[keys, :], NN)
            dq2_s[...] += dot(ds, k_s[keys, :], NN)
            dk_s[keys, :] += dot(ds, q2_s[...], TN)
            dv_s[keys, :] += dot(p, do2_s[...], TN)
            return c

        lax.fori_loop(low, i + 1, apply, 0)
        o_ref[rows, :] = jnp.where(lane < HD, o2_s[:BLOCK, :], o2_s[BLOCK:, :]).astype(BF16)
        dq = jnp.where(lane < HD, dq2_s[:BLOCK, :], dq2_s[BLOCK:, :]) * (1.0 / math.sqrt(HD))
        da_ref[0, rows, :] = (dq * cos_ref[rows, :] - turn(dq) * sin_ref[rows, :]).astype(BF16)
        return carry

    lax.fori_loop(0, blocks, query_block, 0)

    def finish(b, carry):
        rows = pl.ds(pl.multiple_of(b * BLOCK, BLOCK), BLOCK)
        dk = dk_s[rows, :]
        da_ref[1, rows, :] = (dk * cos_ref[rows, :] - turn(dk) * sin_ref[rows, :]).astype(BF16)
        da_ref[2, rows, :] = dv_s[rows, :].astype(BF16)
        return carry

    lax.fori_loop(0, blocks, finish, 0)


def attention(low, projected, back, start, cosine, sine):
    _, slots, width = projected.shape
    pairs = width // PAIR
    span = MAXLEN // BLOCK + 1
    return pl.pallas_call(
        attention_kernel,
        grid_spec=pltpu.PrefetchScalarGridSpec(
            num_scalar_prefetch=1,
            grid=(pairs,),
            in_specs=[
                pl.BlockSpec((3, slots, PAIR), lambda g, low: (0, 0, g)),
                pl.BlockSpec((slots, PAIR), lambda g, low: (0, g)),
                pl.BlockSpec((slots, 1), lambda g, low: (0, 0)),
                pl.BlockSpec((slots, PAIR), lambda g, low: (0, 0)),
                pl.BlockSpec((slots, PAIR), lambda g, low: (0, 0)),
            ],
            out_specs=[
                pl.BlockSpec((slots, PAIR), lambda g, low: (0, g)),
                pl.BlockSpec((3, slots, PAIR), lambda g, low: (0, 0, g)),
            ],
            scratch_shapes=[
                pltpu.VMEM((slots, PAIR), BF16),
                pltpu.VMEM((slots, PAIR), BF16),
                pltpu.VMEM((slots, PAIR), BF16),
                pltpu.VMEM((slots, PAIR), F32),
                pltpu.VMEM((slots, PAIR), F32),
                pltpu.VMEM((span, 2 * BLOCK, BLOCK), F32),
                pltpu.VMEM((span, 2 * BLOCK, BLOCK), F32),
                pltpu.VMEM((2 * BLOCK, PAIR), BF16),
                pltpu.VMEM((2 * BLOCK, PAIR), BF16),
                pltpu.VMEM((2 * BLOCK, PAIR), F32),
                pltpu.VMEM((2 * BLOCK, PAIR), F32),
                pltpu.VMEM((2 * BLOCK, PAIR), F32),
                pltpu.VMEM((2 * BLOCK, PAIR), F32),
                pltpu.VMEM((2 * BLOCK, PAIR), F32),
            ],
        ),
        out_shape=[
            jax.ShapeDtypeStruct((slots, width), BF16),
            jax.ShapeDtypeStruct((3, slots, width), BF16),
        ],
        compiler_params=pltpu.CompilerParams(vmem_limit_bytes=52 * 2**20),
        cost_estimate=pl.CostEstimate(
            flops=24 * slots * MAXLEN * width, bytes_accessed=24 * slots * width,
            transcendentals=slots * MAXLEN * width // HD,
        ),
        name="attention",
    )(low, projected, back, start, cosine, sine)


def feed_kernel(h_ref, dy_ref, up_ref, bias_ref, down_ref,
                part_ref, dh_ref, dup_ref, dbias_ref, ddown_ref, up_s, down_s, part_s, dh_s):
    slots = h_ref.shape[0]
    step = pl.program_id(0)
    last = pl.num_programs(0) - 1
    up_s[...] = jnp.zeros(up_s.shape, F32)
    down_s[...] = jnp.zeros(down_s.shape, F32)
    dbias_ref[...] = jnp.zeros(dbias_ref.shape, F32)

    @pl.when(step == 0)
    def _():
        part_s[...] = jnp.zeros(part_s.shape, F32)
        dh_s[...] = jnp.zeros(dh_s.shape, F32)

    def body(b, carry):
        rows = pl.ds(pl.multiple_of(b * ROWS, ROWS), ROWS)
        h = h_ref[rows, :]
        dy = dy_ref[rows, :]
        u = dot(h, up_ref[...], NN) + bias_ref[...].astype(F32)
        dg = dot(dy, down_ref[...], NT)
        phi = 0.5 * (1.0 + lax.erf(u * math.sqrt(0.5)))
        g = (u * phi).astype(BF16)
        slope = phi + u * (jnp.exp(-0.5 * (u * u)) * (1.0 / math.sqrt(2.0 * math.pi)))
        du = (slope * dg).astype(BF16)
        part_s[rows, :] += dot(g, down_ref[...], NN)
        down_s[...] += dot(g, dy, TN)
        dh_s[rows, :] += dot(du, up_ref[...], NT)
        up_s[...] += dot(h, du, TN)
        dbias_ref[...] += jnp.sum(du.astype(F32), 0, keepdims=True)
        return carry

    lax.fori_loop(0, slots // ROWS, body, 0)
    dup_ref[...] = up_s[...].astype(dup_ref.dtype)
    ddown_ref[...] = down_s[...].astype(ddown_ref.dtype)

    @pl.when(step == last)
    def _():
        part_ref[...] = part_s[...].astype(part_ref.dtype)
        dh_ref[...] = dh_s[...].astype(dh_ref.dtype)


def feed(h, dy, up, bias, down):
    slots, width = h.shape
    hidden = up.shape[1]
    tile = 256
    whole = lambda t: (0, 0)
    return pl.pallas_call(
        feed_kernel,
        grid=(hidden // tile,),
        in_specs=[
            pl.BlockSpec((slots, width), whole, pipeline_mode=pl.Buffered(1)),
            pl.BlockSpec((slots, width), whole, pipeline_mode=pl.Buffered(1)),
            pl.BlockSpec((width, tile), lambda t: (0, t)),
            pl.BlockSpec((1, tile), lambda t: (0, t)),
            pl.BlockSpec((tile, width), lambda t: (t, 0)),
        ],
        out_specs=[
            pl.BlockSpec((slots, width), whole, pipeline_mode=pl.Buffered(1)),
            pl.BlockSpec((slots, width), whole, pipeline_mode=pl.Buffered(1)),
            pl.BlockSpec((width, tile), lambda t: (0, t)),
            pl.BlockSpec((1, tile), lambda t: (0, t)),
            pl.BlockSpec((tile, width), lambda t: (t, 0)),
        ],
        scratch_shapes=[
            pltpu.VMEM((width, tile), F32),
            pltpu.VMEM((tile, width), F32),
            pltpu.VMEM((slots, width), F32),
            pltpu.VMEM((slots, width), F32),
        ],
        out_shape=[
            jax.ShapeDtypeStruct((slots, width), F32),
            jax.ShapeDtypeStruct((slots, width), F32),
            jax.ShapeDtypeStruct((width, hidden), BF16),
            jax.ShapeDtypeStruct((1, hidden), F32),
            jax.ShapeDtypeStruct((hidden, width), BF16),
        ],
        compiler_params=pltpu.CompilerParams(vmem_limit_bytes=56 * 2**20),
        cost_estimate=pl.CostEstimate(
            flops=12 * slots * width * hidden, bytes_accessed=22 * 2**20,
            transcendentals=2 * slots * hidden,
        ),
        name="feed",
    )(h, dy, up, bias, down)


def exchange_kernel(near, far, x_ref, out_ref, held, mid, far_held, total, send, recv):
    me = lax.axis_index("dp")
    inner = lax.rem(me, near)
    outer = me // near

    def at_near(d):
        return outer * near + lax.rem(inner + d, near)

    def at_far(d):
        return lax.rem(outer + d, far) * near + inner

    def copy(source, target, phase, d, device):
        return pltpu.make_async_remote_copy(
            src_ref=source,
            dst_ref=target,
            send_sem=send.at[phase, d],
            recv_sem=recv.at[phase, d],
            device_id={"dp": device},
            device_id_type=pl.DeviceIdType.MESH,
        )

    def one(d):
        return copy(x_ref.at[lax.rem(inner + d, near)], held.at[d], 0, d, at_near(d))

    def two(d):
        return copy(mid.at[lax.rem(outer + d, far)], far_held.at[d], 1, d, at_far(d))

    def three(d):
        return copy(out_ref.at[inner, outer], out_ref.at[inner, outer], 2, d, at_far(d))

    def four(d):
        return copy(out_ref.at[inner], out_ref.at[inner], 3, d, at_near(d))

    def each(stop, action):
        def body(d, c):
            action(d)
            return c

        lax.fori_loop(1, stop, body, 0)

    barrier = pltpu.get_barrier_semaphore()

    def greet(device):
        pl.semaphore_signal(
            barrier, inc=1, device_id={"dp": device}, device_id_type=pl.DeviceIdType.MESH
        )

    each(near, lambda d: greet(at_near(d)))
    each(far, lambda d: greet(at_far(d)))
    pl.semaphore_wait(barrier, near + far - 2)

    each(near, lambda d: one(d).start())
    each(near, lambda d: one(d).wait_recv())

    def fold(o, c):
        value = x_ref[inner, o].astype(F32)
        for d in range(1, near):
            value = value + held[d, o].astype(F32)
        mid[o] = value.astype(BF16)
        return c

    lax.fori_loop(0, far, fold, 0)
    each(far, lambda d: two(d).start())
    total[...] = mid[outer].astype(F32)

    def take(d):
        two(d).wait_recv()
        total[...] += far_held[d].astype(F32)

    each(far, take)
    out_ref[inner, outer] = total[...].astype(BF16)
    each(far, lambda d: three(d).start())
    each(far, lambda d: three(d).wait_recv())
    each(near, lambda d: four(d).start())
    each(near, lambda d: four(d).wait_recv())
    each(near, lambda d: one(d).wait_send())
    each(far, lambda d: two(d).wait_send())
    each(far, lambda d: three(d).wait_send())
    each(near, lambda d: four(d).wait_send())


def exchange(parts):
    count, chunk, cols = parts.shape
    near = 4
    far = count // near
    shape = (near, far, chunk, cols)
    return pl.pallas_call(
        functools.partial(exchange_kernel, near, far),
        out_shape=jax.ShapeDtypeStruct(shape, BF16),
        in_specs=[pl.BlockSpec(memory_space=pltpu.VMEM)],
        out_specs=pl.BlockSpec(memory_space=pltpu.VMEM),
        scratch_shapes=[
            pltpu.VMEM(shape, BF16),
            pltpu.VMEM((far, chunk, cols), BF16),
            pltpu.VMEM((far, chunk, cols), BF16),
            pltpu.VMEM((chunk, cols), F32),
            pltpu.SemaphoreType.DMA((4, max(near, far))),
            pltpu.SemaphoreType.DMA((4, max(near, far))),
        ],
        compiler_params=pltpu.CompilerParams(
            collective_id=0, has_side_effects=True, vmem_limit_bytes=32 * 2**20
        ),
        name="exchange",
    )(parts.reshape(shape))


def shards(
    tokens,
    out_cot,
    norm_gain,
    norm_bias,
    qkv_weight,
    qkv_bias,
    out_weight,
    out_bias,
    up_weight,
    up_bias,
    down_weight,
    seq_lengths,
    seq_owner,
):
    rows_local = tokens.shape[0]
    slots = rows_local * lax.axis_size("tensor")
    half_index = lax.axis_index("tensor")
    start, filled = layout(seq_lengths, seq_owner, lax.axis_index("dp"), slots)
    places = jnp.arange(slots, dtype=jnp.int32) - start
    valid_local = lax.dynamic_slice_in_dim(filled, half_index * rows_local, rows_local, 0)
    gains = norm_gain.astype(F32)
    shifts = norm_bias.astype(F32)
    x = tokens.astype(F32)
    whole_rows = lax.all_gather(tokens, "tensor", axis=0, tiled=True)
    cot_local = out_cot * valid_local[:, None].astype(BF16)
    cot = lax.all_gather(cot_local, "tensor", axis=0, tiled=True)
    unit_rows, inverse_rows = standard(whole_rows.astype(F32))
    first = (unit_rows * gains[0] + shifts[0]).astype(BF16)
    second = (unit_rows * gains[1] + shifts[1]).astype(BF16)

    feed_part, second_back, up_grad, up_bias_grad, down_grad = feed(
        second, cot, up_weight, up_bias[None, :], down_weight
    )
    up_sum, down_sum = lax.psum((up_grad, down_grad), "dp")

    projected = (
        jnp.einsum("sd,cde->cse", first, qkv_weight, preferred_element_type=F32)
        + qkv_bias.astype(F32)[:, None, :]
    )
    attended_back = dot(cot, out_weight, NT).astype(BF16)
    cosine, sine = rotary_tables(places)
    attended, qkv_delta = attention(
        start[::BLOCK] // BLOCK, projected, attended_back, start[:, None], cosine, sine
    )

    partial_value = feed_part + dot(attended, out_weight, NN)
    summed = lax.psum_scatter(
        partial_value.astype(BF16), "tensor", scatter_dimension=0, tiled=True
    ).astype(F32)
    biases = out_bias.astype(F32)
    mixed = (x + summed + biases[0] + biases[1]).astype(BF16)
    out_w_grad = dot(attended, cot, TN)
    qkv_grad = jnp.einsum("sd,cse->cde", first, qkv_delta, preferred_element_type=F32)
    qkv_bias_grad = jnp.sum(qkv_delta.astype(F32), 1)
    first_back = jnp.einsum("cse,cde->sd", qkv_delta, qkv_weight, preferred_element_type=F32)
    combined = gains[0] * first_back + gains[1] * second_back
    combined_sum = lax.psum_scatter(
        combined.astype(BF16), "tensor", scatter_dimension=0, tiled=True
    ).astype(F32)

    gain_grad = jnp.stack(
        [jnp.sum(first_back * unit_rows, 0), jnp.sum(second_back * unit_rows, 0)], 0
    )
    shift_grad = jnp.stack([jnp.sum(first_back, 0), jnp.sum(second_back, 0)], 0)
    bias_grad = jnp.sum(cot_local.astype(F32), 0)

    width = tokens.shape[1]
    shared = jnp.concatenate([gain_grad, shift_grad, bias_grad[None]], 0).reshape(-1)
    shared = lax.psum(shared, "tensor")
    vectors = jnp.concatenate([shared, qkv_bias_grad.reshape(-1), up_bias_grad.reshape(-1)])
    cols = qkv_grad.shape[2]
    extra = -(-vectors.size // cols)
    vectors = jnp.pad(vectors, (0, extra * cols - vectors.size)).reshape(extra, cols)
    qkv_rows = qkv_grad.shape[0] * qkv_grad.shape[1]
    out_rows = out_w_grad.shape[0]
    pieces = [qkv_grad.reshape(qkv_rows, cols)]
    pieces += [out_w_grad[:, c : c + cols] for c in range(0, width, cols)]
    pieces += [vectors]
    count = lax.axis_size("dp")
    used = sum(piece.shape[0] for piece in pieces)
    chunk = -(-used // (16 * count)) * 16
    pieces += [jnp.zeros((chunk * count - used, cols), F32)]
    joined = jnp.concatenate([piece.astype(BF16) for piece in pieces], 0)
    total = exchange(joined.reshape(count, chunk, cols)).reshape(chunk * count, cols)
    qkv_sum = total[:qkv_rows].reshape(qkv_grad.shape)
    out_sum = jnp.concatenate(
        [
            total[qkv_rows + n * out_rows : qkv_rows + (n + 1) * out_rows]
            for n in range(width // cols)
        ],
        1,
    )
    vector_sum = total[used - extra : used].astype(F32).reshape(-1)
    shared_sum = vector_sum[: 5 * width].reshape(5, width)
    qkv_bias_sum = vector_sum[5 * width : 5 * width + qkv_bias.size].reshape(qkv_bias.shape)
    up_bias_sum = vector_sum[5 * width + qkv_bias.size :][: up_bias.size]

    unit_local = lax.dynamic_slice_in_dim(unit_rows, half_index * rows_local, rows_local, 0)
    inverse_local = lax.dynamic_slice_in_dim(inverse_rows, half_index * rows_local, rows_local, 0)
    average = jnp.mean(combined_sum, -1, keepdims=True)
    along = jnp.mean(combined_sum * unit_local, -1, keepdims=True)
    x_back = inverse_local * (combined_sum - average - unit_local * along)
    tokens_grad = (cot_local.astype(F32) + x_back).astype(BF16)
    return (
        mixed,
        tokens_grad,
        shared_sum[:2],
        shared_sum[2:4],
        qkv_sum.astype(F32),
        qkv_bias_sum,
        out_sum.astype(F32),
        jnp.stack([shared_sum[4], shared_sum[4]], 0),
        up_sum.astype(F32),
        up_bias_sum,
        down_sum.astype(F32),
    )

def solution(mesh):
    return jax.shard_map(
        shards,
        mesh=mesh,
        in_specs=(
            P(("dp", "tensor"), None),
            P(("dp", "tensor"), None),
            P(),
            P(),
            P(None, None, "tensor"),
            P(None, "tensor"),
            P("tensor", None),
            P(),
            P(None, "tensor"),
            P("tensor"),
            P("tensor", None),
            P(),
            P(),
        ),
        out_specs=(
            P(("dp", "tensor"), None),
            P(("dp", "tensor"), None),
            P(),
            P(),
            P(None, None, "tensor"),
            P(None, "tensor"),
            P("tensor", None),
            P(),
            P(None, "tensor"),
            P("tensor"),
            P("tensor", None),
        ),
        check_vma=False,
    )
```
